1024 devices in a mesh: expert: 16 (over z, x_hi), dp: 64 (over x_lo, y, core).
Axes of the slice: x: 8 (x_hi: 2, x_lo: 4; x = x_hi * 4 + x_lo), y: 8, z: 8, core: 2. Of those that a mesh axis runs over, the one named last changes fastest.
Arguments:
- grad_out: bfloat16 [2048, 4096], P('dp', 'expert'), may hold values from -6 to 6
- gate_prob: float32 [2048, 8], P('dp'), may hold values from 0.05 to 1
- routes: int32 [2048, 8], P('dp'), may hold values from 0 to 63, all different within a row; in each aligned block of 32 rows (0 to 31, 32 to 63, ...) at most 8 rows name the same one
- slot_expert: int32 [64], replicated, may hold values from 0 to 62, as said below
- saved_input: bfloat16 [64, 512, 4096], P('dp', None, 'expert'), may hold values from -6 to 6
- gate_weight: bfloat16 [64, 4096, 1024], P('dp', 'expert'), as said below
- up_weight: bfloat16 [64, 4096, 1024], P('dp', 'expert'), as said below
- down_weight: bfloat16 [64, 1024, 4096], P('dp', None, 'expert'), as said below
Outputs:
- grad_input: bfloat16 [2048, 4096], P('dp', 'expert')
- grad_gate_w: bfloat16 [64, 4096, 1024], P('dp', 'expert')
- grad_up_w: bfloat16 [64, 4096, 1024], P('dp', 'expert')
- grad_down_w: bfloat16 [64, 1024, 4096], P('dp', None, 'expert')
The draws below stay inside these ranges and needn't reach their ends.
Inputs may be any that keep to these rules, and one draw needn't show every extreme that they name: `routes`: each row names 8 different slots; in the rows of one dp index (32 aligned rows) no slot is named by more than 8 rows, a bound that some block reaches. `slot_expert`: slots s and s + 32 form a pair; the two slots of a pair serve one expert or two experts that no other slot serves; slots 0 and 32 serve one expert, the other pairs vary. `gate_weight`: the two slots of a pair that serve one expert hold equal weights. `up_weight`: the two slots of a pair that serve one expert hold equal weights. `down_weight`: the two slots of a pair that serve one expert hold equal weights.
All inputs are finite; a program needn't handle non-finite values.
Results may differ from the reference program's by a relative error of at most 0.03.
Values may be sent and summed in bfloat16 or wider, within the bound.
A program may use at most 32 MiB of HBM per device.

```python
import math
import jax
import jax.numpy as jnp
import numpy as np
from jax import lax

D = 4096
F = 1024
TOK_DEV = 32
TOP = 8
CAP = 8
EXPERTS = 63
TOKENS = 2048
N_EXPERT = 16
N_DP = 64


def placement(key):
    key = jax.random.fold_in(key, 101)
    half_count = N_DP // 2
    first_key, second_key = jax.random.split(key)
    coins = jax.random.randint(first_key, (half_count,), 0, 2).astype(jnp.int32)
    paired = jnp.where(jnp.arange(half_count, dtype=jnp.int32) == 0, 1, coins).astype(jnp.int32)
    lower_ids = jnp.arange(half_count, dtype=jnp.int32)
    fresh_ids = half_count + jnp.cumsum(1 - paired) - 1
    upper_ids = jnp.where(paired == 1, lower_ids, fresh_ids).astype(jnp.int32)
    rest = jax.random.permutation(second_key, EXPERTS - 1).astype(jnp.int32)
    labels = jnp.concatenate([jnp.array([EXPERTS - 1], jnp.int32), rest])
    return labels[jnp.concatenate([lower_ids, upper_ids])].astype(jnp.int32)


def paired_weights(key, table, rows, cols, scale):
    half_count = N_DP // 2
    lower_key, upper_key = jax.random.split(key)
    lower = jax.random.normal(lower_key, (half_count, rows, cols), jnp.float32) * scale
    upper = jax.random.normal(upper_key, (half_count, rows, cols), jnp.float32) * scale
    same = table[:half_count] == table[half_count:]
    upper = jnp.where(same[:, None, None], lower, upper)
    return jnp.concatenate([lower, upper], axis=0).astype(jnp.bfloat16)


def draw_slot_expert(key, part):
    return placement(key)


def draw_gate_weight(key, part):
    table = placement(key)
    key = jax.random.fold_in(key, 7)
    return paired_weights(key, table, D, F, D ** (-0.5))


def draw_up_weight(key, part):
    table = placement(key)
    key = jax.random.fold_in(key, 8)
    return paired_weights(key, table, D, F, D ** (-0.5))


def draw_down_weight(key, part):
    table = placement(key)
    key = jax.random.fold_in(key, 9)
    return paired_weights(key, table, F, D, F ** (-0.5))


def block_scale(own_key, shape, cuts, low, high):
    def one(dim, parts):
        heights = jax.random.uniform(jax.random.fold_in(jax.random.fold_in(own_key, 6), dim), (parts,), jnp.float32, low / len(cuts), high / len(cuts))
        return jnp.repeat(jnp.exp(heights), shape[dim] // parts).reshape((-1,) + (1,) * (len(shape) - dim - 1))

    gain = one(*cuts[0])
    for cut in cuts[1:]:
        gain = gain * one(*cut)
    return gain


def assign_block(rng, own, number, rows, number_of, top, most, lean):
    ranking = jax.random.permutation(rng, number_of)
    crowded, usual = load_shares(number_of, rows * top, most, lean, True), load_shares(number_of, rows * top, most, lean, False)
    places = jnp.arange(number_of)

    def named(lengths, turn):
        used = int((lengths > 0).sum())
        fixed = max(1, used // 4)
        passed = fixed + (places - fixed + turn * (used - fixed)) % max(1, number_of - fixed)
        return jnp.zeros((number_of,), jnp.int32).at[ranking[jnp.where(places < fixed, places, passed)]].set(jnp.asarray(lengths, jnp.int32))

    lengths = jnp.where(number % 4 == 0, named(crowded, number // 4), named(usual, number - number // 4 - 1))
    mixed = jax.random.permutation(jax.random.fold_in(own, 3), number_of)
    source_of, taker = mixed[0:number_of // 2 * 2:2], mixed[1:number_of // 2 * 2:2]
    margin = jnp.minimum(lengths[source_of] - 1, most - lengths[taker]) // 2
    margin = jnp.where((source_of == ranking[0]) | (taker == ranking[0]) | (lengths[taker] == 0), 0, jnp.maximum(margin, 0))
    passed = jax.random.randint(jax.random.fold_in(own, 4), (number_of // 2,), 0, 1 << 20) % (margin + 1)
    lengths = lengths.at[source_of].add(-passed).at[taker].add(passed)
    items = jnp.searchsorted(jnp.cumsum(lengths), jnp.arange(rows * top), side="right").astype(jnp.int32)
    listing = items.reshape(top, rows).T
    listing = listing[jax.random.permutation(jax.random.fold_in(own, 1), rows)]
    turn = jax.random.randint(jax.random.fold_in(own, 2), (rows, 1), 0, top)
    return jnp.take_along_axis(listing, (jnp.arange(top)[None, :] + turn) % top, axis=1)


def load_shares(count, total, limit, slope, full):
    loads = [(1 << 20) // math.isqrt(rank ** slope) + 1 for rank in range(1, count + 1)]
    largest = limit if full else min(limit, max(-(-total // count), total * loads[0] // sum(loads)))
    least = 1 if total - largest >= count - 1 else 0
    holding, spare = [largest] + [least] * (count - 1), total - largest - least * (count - 1)
    while spare > 0:
        free = [i for i in range(1, count) if holding[i] < largest] or [i for i in range(1, count) if holding[i] < limit]
        mass, left = sum([loads[i] for i in free]), spare
        for i in free:
            extra = min(limit - holding[i], max(1, left * loads[i] // mass), spare)
            holding[i] = holding[i] + extra
            spare = spare - extra
    return np.array(holding)


def bell_draw(rng, extent, deviation, limit, cuts=(), held_as=jnp.bfloat16):
    result = deviation * jax.random.normal(rng, extent, jnp.float32)
    if cuts:
        result = result * block_scale(rng, extent, cuts, -0.22, 0.18)
    return jnp.clip(result, -limit, limit).astype(held_as)


def setup_inputs(seed: int = 0) -> dict:
    key_of = jax.random.split(jax.random.key(seed), 9)
    grad_out = bell_draw(key_of[0], (TOKENS, D), 1.0, 6.0, ((0, 64), (1, 16)))
    gate_prob = jnp.clip(jnp.exp(math.log(1.0) - 2.9957323 * jax.random.uniform(key_of[1], (TOKENS, TOP), jnp.float32) ** block_scale(key_of[1], (TOKENS, TOP), ((0, 64),), -0.2, 0.2)), 0.05, 1.0)
    routes_keys = jax.random.split(jax.random.fold_in(key_of[2], 1), TOKENS // TOK_DEV)
    routes_turns = jax.random.permutation(jax.random.fold_in(key_of[2], 3), TOKENS // TOK_DEV)
    routes = jax.vmap(lambda own, number: assign_block(jax.random.fold_in(key_of[2], 2), own, number, TOK_DEV, N_DP, TOP, CAP, 2))(routes_keys, routes_turns).reshape((TOKENS, TOP))
    slot_expert = draw_slot_expert(jax.random.fold_in(key_of[8], 71), 0)
    saved_input = bell_draw(key_of[4], (N_DP, N_DP * CAP, D), 1.0, 6.0, ((0, 64), (2, 16)))
    gate_weight = draw_gate_weight(jax.random.fold_in(key_of[8], 71), 0)
    up_weight = draw_up_weight(jax.random.fold_in(key_of[8], 71), 0)
    down_weight = draw_down_weight(jax.random.fold_in(key_of[8], 71), 0)
    return dict(grad_out=grad_out, gate_prob=gate_prob, routes=routes, slot_expert=slot_expert, saved_input=saved_input, gate_weight=gate_weight, up_weight=up_weight, down_weight=down_weight)


def contract(left, right, left_dim, right_dim):
    return lax.dot_general(left, right, (((left_dim,), (right_dim,)), ((), ())), preferred_element_type=jnp.float32)


def block_sum(rows, weight_blocks):
    pieces = rows.astype(jnp.float32).reshape(rows.shape[0], N_EXPERT, -1)
    terms = jnp.einsum('rbd,bdf->brf', pieces, weight_blocks.astype(jnp.float32))
    rounded = lax.optimization_barrier(terms.astype(jnp.bfloat16))
    return jnp.sum(rounded.astype(jnp.float32), axis=0)


def slot_backward(grad_rows, inputs, gate_w, up_w, down_w):
    hidden_count = gate_w.shape[1]
    gate_pre = block_sum(inputs, gate_w.reshape(N_EXPERT, -1, hidden_count))
    up_pre = block_sum(inputs, up_w.reshape(N_EXPERT, -1, hidden_count))
    down_blocks = jnp.transpose(down_w.reshape(hidden_count, N_EXPERT, -1), (1, 2, 0))
    grad_act = block_sum(grad_rows, down_blocks)
    sigmoid_gate = jax.nn.sigmoid(gate_pre)
    gated = gate_pre * sigmoid_gate
    activated = (gated * up_pre).astype(jnp.bfloat16)
    grad_up = (grad_act * gated).astype(jnp.bfloat16)
    grad_gate = (grad_act * up_pre * sigmoid_gate * (1.0 + gate_pre * (1.0 - sigmoid_gate))).astype(jnp.bfloat16)
    part_gate = contract(inputs, grad_gate, 0, 0)
    part_up = contract(inputs, grad_up, 0, 0)
    part_down = contract(activated, grad_rows, 0, 0)
    returned = (contract(grad_gate, gate_w, 1, 1) + contract(grad_up, up_w, 1, 1)).astype(jnp.bfloat16)
    return returned, part_gate, part_up, part_down


def add_partner(own, other, shared):
    rounded = lax.optimization_barrier(other.astype(jnp.bfloat16))
    return (own + shared * rounded.astype(jnp.float32)).astype(jnp.bfloat16)


def reference(grad_out, gate_prob, routes, slot_expert, saved_input, gate_weight, up_weight, down_weight):
    half_count = N_DP // 2
    rows_per = TOK_DEV * TOP
    scaled = (gate_prob[:, :, None] * grad_out[:, None, :].astype(jnp.float32)).astype(jnp.bfloat16)
    scaled = scaled.reshape(N_DP, rows_per, D)
    flat_routes = routes.reshape(N_DP, rows_per).astype(jnp.int32)
    chosen = (flat_routes[:, :, None] == jnp.arange(N_DP, dtype=jnp.int32)[None, None, :]).astype(jnp.int32)
    earlier = jnp.cumsum(chosen, axis=1) - chosen
    position = jnp.sum(earlier * chosen, axis=2).astype(jnp.int32)
    source = jnp.broadcast_to(jnp.arange(N_DP, dtype=jnp.int32)[:, None], (N_DP, rows_per))
    grad_rows = jnp.zeros((N_DP, N_DP, CAP, D), jnp.bfloat16).at[flat_routes, source, position].set(scaled)
    grad_rows = grad_rows.reshape(N_DP, N_DP * CAP, D)

    def pair_step(index):
        upper_index = index + half_count
        lower = slot_backward(grad_rows[index], saved_input[index], gate_weight[index], up_weight[index], down_weight[index])
        upper = slot_backward(grad_rows[upper_index], saved_input[upper_index], gate_weight[upper_index], up_weight[upper_index], down_weight[upper_index])
        shared = (slot_expert[index] == slot_expert[upper_index]).astype(jnp.float32)
        results = [lower[0], upper[0]]
        for which in range(1, 4):
            results.append(add_partner(lower[which], upper[which], shared))
            results.append(add_partner(upper[which], lower[which], shared))
        return tuple(results)

    outputs = lax.map(pair_step, jnp.arange(half_count, dtype=jnp.int32))
    returned = jnp.concatenate([outputs[0], outputs[1]], axis=0).reshape(N_DP, N_DP, CAP, D)
    grad_gate_w = jnp.concatenate([outputs[2], outputs[3]], axis=0)
    grad_up_w = jnp.concatenate([outputs[4], outputs[5]], axis=0)
    grad_down_w = jnp.concatenate([outputs[6], outputs[7]], axis=0)
    picked = returned[flat_routes, source, position].astype(jnp.float32)
    grad_input = jnp.sum(picked.reshape(TOKENS, TOP, D), axis=1).astype(jnp.bfloat16)
    return grad_input, grad_gate_w, grad_up_w, grad_down_w
```

```python
import jax
import jax.numpy as jnp
from jax import lax
from jax.experimental import pallas as pl
from jax.experimental.pallas import tpu as pltpu
from jax.sharding import PartitionSpec as P

MESH = pl.DeviceIdType.MESH
GATE, UP, ACT = 0, 1, 2


def contract(left, right, left_dim, right_dim):
    return lax.dot_general(
        left, right, (((left_dim,), (right_dim,)), ((), ())), preferred_element_type=jnp.float32
    )


def slot_kernel(
    shared_ref,
    x_ref,
    rows_ref,
    gate_ref,
    up_ref,
    down_ref,
    returned_ref,
    grad_gate_ref,
    grad_up_ref,
    grad_down_ref,
    ring,
    own,
    swap_out,
    swap_in,
    full,
    other,
    x_other,
    down_out,
    down_in,
    ring_send,
    ring_recv,
    swap_send,
    swap_recv,
    full_send,
    full_recv,
    other_send,
    other_recv,
    pair_send,
    pair_recv,
    x_send,
    x_recv,
    down_send,
    down_recv,
):
    e = lax.axis_index("expert")
    d = lax.axis_index("dp")
    nz = lax.axis_size("expert") // 2
    ndp = lax.axis_size("dp")
    z, h = e // 2, e % 2
    rows = x_ref.shape[0] // nz
    half = gate_ref.shape[1] // 2
    step_of = (1, nz - 1)
    to = tuple((((z + k) % nz) * 2 + h, d) for k in step_of)
    twin = (z * 2 + (1 - h), d)
    pair = (e, (d + ndp // 2) % ndp)

    barrier = pltpu.get_barrier_semaphore()
    for device in (to[0], to[1], twin, pair):
        pl.semaphore_signal(barrier, inc=1, device_id=device, device_id_type=MESH)
    pl.semaphore_wait(barrier, 4)

    def remote(src, dst, send, recv, device):
        return pltpu.make_async_remote_copy(
            src_ref=src, dst_ref=dst, send_sem=send, recv_sem=recv, device_id=device, device_id_type=MESH
        )

    def block(index):
        return pl.ds(pl.multiple_of(index * rows, rows), rows)

    def term(a, way, index):
        cols = pl.ds(way * half, half)
        if a == GATE:
            return contract(x_ref[block(index), :], gate_ref[:, cols], 1, 0)
        if a == UP:
            return contract(x_ref[block(index), :], up_ref[:, cols], 1, 0)
        return contract(rows_ref[block(index), :], down_ref[cols, :], 1, 1)

    def ring_copy(a, way, s):
        return remote(
            ring.at[a, way, s], ring.at[a, way, s + 1], ring_send.at[a, way, s], ring_recv.at[a, way, s], to[way]
        )

    def chunk(way, s):
        return (z + (nz - 1 - s if way == 0 else 1 + s)) % nz

    everything = [(a, way) for a in (GATE, UP, ACT) for way in (0, 1)]
    for a, way in everything:
        ring[a, way, 0] = term(a, way, chunk(way, 0)).astype(jnp.bfloat16)
        ring_copy(a, way, 0).start()
    x_copy = remote(x_ref, x_other, x_send, x_recv, pair)
    x_copy.start()

    def ring_step(s, carry):
        for a, way in everything:
            mine = term(a, way, chunk(way, s + 1))
            ring_copy(a, way, s).wait_recv()
            ring[a, way, s + 1] = (ring[a, way, s + 1].astype(jnp.float32) + mine).astype(jnp.bfloat16)
            ring_copy(a, way, s + 1).start()
        return carry

    lax.fori_loop(0, nz - 2, ring_step, 0)

    def swap_copy(a, way):
        return remote(swap_out.at[a, way], swap_in.at[a, way], swap_send.at[a, way], swap_recv.at[a, way], twin)

    for a, way in everything:
        mine = term(a, way, z)
        ring_copy(a, way, nz - 2).wait_recv()
        total = ring[a, way, nz - 1].astype(jnp.float32) + mine
        own[a, way] = total
        swap_out[a, way] = total.astype(jnp.bfloat16)
        swap_copy(a, way).start()

    def full_copy(a, way, s):
        at = block((z + (nz - s if way == 0 else s)) % nz)
        return remote(
            full.at[a, way, at, :], full.at[a, way, at, :], full_send.at[a, way, s], full_recv.at[a, way, s], to[way]
        )

    def other_copy(a, way, s):
        at = block((z + (nz - s if way == 0 else s)) % nz)
        return remote(
            other.at[a, way, at, :],
            other.at[a, way, at, :],
            other_send.at[a, way, s],
            other_recv.at[a, way, s],
            to[way],
        )

    def pair_copy(a, way):
        at = block(z)
        return remote(
            full.at[a, way, at, :], other.at[a, way, at, :], pair_send.at[a, way], pair_recv.at[a, way], pair
        )

    for way in (0, 1):
        value = []
        for a in (GATE, UP, ACT):
            swap_copy(a, way).wait_recv()
            value.append(own[a, way] + swap_in[a, way].astype(jnp.float32))
        gate_pre, up_pre, grad_act = value
        sigmoid_gate = jax.nn.sigmoid(gate_pre)
        gated = gate_pre * sigmoid_gate
        full[ACT, way, block(z), :] = (gated * up_pre).astype(jnp.bfloat16)
        full_copy(ACT, way, 0).start()
        full[GATE, way, block(z), :] = (
            grad_act * up_pre * sigmoid_gate * (1.0 + gate_pre * (1.0 - sigmoid_gate))
        ).astype(jnp.bfloat16)
        full_copy(GATE, way, 0).start()
        full[UP, way, block(z), :] = (grad_act * gated).astype(jnp.bfloat16)
        full_copy(UP, way, 0).start()
        pair_copy(GATE, way).start()
        pair_copy(UP, way).start()

    def full_step(s, carry):
        for a in (ACT, GATE, UP):
            for way in (0, 1):
                full_copy(a, way, s).wait_recv()
                full_copy(a, way, s + 1).start()
        return carry

    lax.fori_loop(0, nz - 2, full_step, 0)

    for a in (GATE, UP):
        for way in (0, 1):
            pair_copy(a, way).wait_recv()
            other_copy(a, way, 0).start()

    down_copy = [
        remote(down_out.at[way], down_in.at[way], down_send.at[way], down_recv.at[way], pair) for way in (0, 1)
    ]
    for way in (0, 1):
        full_copy(ACT, way, nz - 2).wait_recv()
        part = contract(full[ACT, way], rows_ref[...], 0, 0)
        grad_down_ref[pl.ds(way * half, half), :] = part.astype(jnp.bfloat16)
        down_out[way] = part.astype(jnp.bfloat16)
        down_copy[way].start()
    for a in (GATE, UP):
        for way in (0, 1):
            full_copy(a, way, nz - 2).wait_recv()
    returned_ref[...] = sum(
        contract(full[a, way], w[:, pl.ds(way * half, half)], 1, 1)
        for a, w in ((GATE, gate_ref), (UP, up_ref))
        for way in (0, 1)
    ).astype(jnp.bfloat16)

    def other_step(s, carry):
        for a in (GATE, UP):
            for way in (0, 1):
                other_copy(a, way, s).wait_recv()
                other_copy(a, way, s + 1).start()
        return carry

    lax.fori_loop(0, nz - 2, other_step, 0)

    x_copy.wait_recv()
    shared = shared_ref[0:1, 0:1]
    for a, out in ((GATE, grad_gate_ref), (UP, grad_up_ref)):
        for way in (0, 1):
            part = contract(x_ref[...], full[a, way], 0, 0)
            other_copy(a, way, nz - 2).wait_recv()
            part = part + shared * contract(x_other[...], other[a, way], 0, 0)
            out[:, pl.ds(way * half, half)] = part.astype(jnp.bfloat16)
    for way in (0, 1):
        at = pl.ds(way * half, half)
        down_copy[way].wait_recv()
        grad_down_ref[at, :] = (
            grad_down_ref[at, :].astype(jnp.float32) + shared * down_in[way].astype(jnp.float32)
        ).astype(jnp.bfloat16)

    x_copy.wait_send()
    for way in (0, 1):
        down_copy[way].wait_send()
        for a in (GATE, UP, ACT):
            swap_copy(a, way).wait_send()
        for a in (GATE, UP):
            pair_copy(a, way).wait_send()

    def drain(s, carry):
        for a, way in everything:
            ring_copy(a, way, s).wait_send()
            full_copy(a, way, s).wait_send()
            if a != ACT:
                other_copy(a, way, s).wait_send()
        return carry

    lax.fori_loop(0, nz - 1, drain, 0)


def slot_call(shared, x, rows, gate_w, up_w, down_w):
    nz = lax.axis_size("expert") // 2
    count, width = x.shape
    hidden = gate_w.shape[1]
    half = hidden // 2
    part = count // nz
    bf16, f32 = jnp.bfloat16, jnp.float32
    vmem = pl.BlockSpec(memory_space=pltpu.VMEM)
    dma = pltpu.SemaphoreType.DMA
    return pl.pallas_call(
        slot_kernel,
        out_shape=(
            jax.ShapeDtypeStruct((count, width), bf16),
            jax.ShapeDtypeStruct((width, hidden), bf16),
            jax.ShapeDtypeStruct((width, hidden), bf16),
            jax.ShapeDtypeStruct((hidden, width), bf16),
        ),
        in_specs=[vmem] * 6,
        out_specs=(vmem,) * 4,
        scratch_shapes=[
            pltpu.VMEM((3, 2, nz, part, half), bf16),
            pltpu.VMEM((3, 2, part, half), f32),
            pltpu.VMEM((3, 2, part, half), bf16),
            pltpu.VMEM((3, 2, part, half), bf16),
            pltpu.VMEM((3, 2, count, half), bf16),
            pltpu.VMEM((2, 2, count, half), bf16),
            pltpu.VMEM((count, width), bf16),
            pltpu.VMEM((2, half, width), bf16),
            pltpu.VMEM((2, half, width), bf16),
            dma((3, 2, nz - 1)),
            dma((3, 2, nz - 1)),
            dma((3, 2)),
            dma((3, 2)),
            dma((3, 2, nz - 1)),
            dma((3, 2, nz - 1)),
            dma((2, 2, nz - 1)),
            dma((2, 2, nz - 1)),
            dma((2, 2)),
            dma((2, 2)),
            dma,
            dma,
            dma((2,)),
            dma((2,)),
        ],
        compiler_params=pltpu.CompilerParams(
            collective_id=0, has_side_effects=True, vmem_limit_bytes=40 * 1024 * 1024
        ),
    )(shared, x, rows, gate_w, up_w, down_w)


def local(
    grad_out, gate_prob, routes, slot_expert, saved_input, gate_weight, up_weight, down_weight
):
    tok_rows, width_part = grad_out.shape
    fanout = routes.shape[1]
    slot_count = lax.axis_size("dp")
    capacity = saved_input.shape[1] // slot_count
    flat_routes = routes.reshape(-1)
    chosen = (flat_routes[:, None] == jnp.arange(slot_count, dtype=jnp.int32)[None, :]).astype(
        jnp.int32
    )
    earlier = jnp.cumsum(chosen, axis=0) - chosen
    position = jnp.sum(earlier * chosen, axis=1)
    target = flat_routes * capacity + position
    select = (
        jnp.arange(slot_count * capacity, dtype=jnp.int32)[:, None] == target[None, :]
    ).astype(jnp.bfloat16)
    scaled = (gate_prob[:, :, None] * grad_out[:, None, :].astype(jnp.float32)).astype(jnp.bfloat16)
    scaled = scaled.reshape(tok_rows * fanout, width_part)
    placed = jnp.dot(select, scaled, preferred_element_type=jnp.float32).astype(jnp.bfloat16)
    arrived = lax.all_to_all(
        placed.reshape(slot_count, capacity, width_part),
        "dp",
        split_axis=0,
        concat_axis=0,
        tiled=True,
    )
    grad_rows = arrived.reshape(slot_count * capacity, width_part)
    my_slot = lax.axis_index("dp")
    partner = (my_slot + slot_count // 2) % slot_count
    shared = (slot_expert[my_slot] == slot_expert[partner]).astype(jnp.float32)
    returned, grad_gate_w, grad_up_w, grad_down_w = slot_call(
        jnp.full((8, 128), shared, jnp.float32),
        saved_input[0],
        grad_rows,
        gate_weight[0],
        up_weight[0],
        down_weight[0],
    )
    back = lax.all_to_all(
        returned.reshape(slot_count, capacity, width_part),
        "dp",
        split_axis=0,
        concat_axis=0,
        tiled=True,
    )
    picked = contract(select, back.reshape(slot_count * capacity, width_part), 0, 0)
    grad_input = jnp.sum(picked.reshape(tok_rows, fanout, width_part), axis=1).astype(jnp.bfloat16)
    return (grad_input, grad_gate_w[None], grad_up_w[None], grad_down_w[None])


def solution(mesh):
    placed = (
        P("dp", "expert"),
        P("dp", None),
        P("dp", None),
        P(),
        P("dp", None, "expert"),
        P("dp", "expert", None),
        P("dp", "expert", None),
        P("dp", None, "expert"),
    )
    return jax.shard_map(
        local,
        mesh=mesh,
        in_specs=placed,
        out_specs=(
            P("dp", "expert"),
            P("dp", "expert", None),
            P("dp", "expert", None),
            P("dp", None, "expert"),
        ),
        check_vma=False,
    )
```

```python
import jax
import jax.numpy as jnp
from jax import lax
from jax.experimental import pallas as pl
from jax.experimental.pallas import tpu as pltpu
from jax.sharding import PartitionSpec as P

MESH = pl.DeviceIdType.MESH
GATE, UP, ACT = 0, 1, 2
FAR = 4
FIRST, SECOND = 2, 4


def contract(left, right, left_dim, right_dim):
    return lax.dot_general(
        left, right, (((left_dim,), (right_dim,)), ((), ())), preferred_element_type=jnp.float32
    )


def slot_kernel(
    shared_ref,
    x_ref,
    placed_ref,
    pick_ref,
    gate_ref,
    up_ref,
    down_ref,
    grad_input_ref,
    grad_gate_ref,
    grad_up_ref,
    grad_down_ref,
    mid,
    arrived,
    rows_ref,
    going,
    mid_back,
    back,
    ring,
    ring_act,
    own,
    swap_out,
    swap_in,
    full,
    other,
    x_other,
    down_out,
    down_in,
    near_send,
    near_recv,
    far_send,
    far_recv,
    back_far_send,
    back_far_recv,
    back_near_send,
    back_near_recv,
    local_sem,
    ring_send,
    ring_recv,
    act_send,
    act_recv,
    swap_send,
    swap_recv,
    full_send,
    full_recv,
    other_send,
    other_recv,
    pair_send,
    pair_recv,
    x_send,
    x_recv,
    down_send,
    down_recv,
):
    e = lax.axis_index("expert")
    d = lax.axis_index("dp")
    nz = lax.axis_size("expert") // 2
    ndp = lax.axis_size("dp")
    far, near = mid.shape[1], mid.shape[0]
    dx, dy = d // near, d % near
    z, h = e // 2, e % 2
    rows = x_ref.shape[0] // nz
    half = gate_ref.shape[1] // 2
    to = tuple((((z + k) % nz) * 2 + h, d) for k in (1, nz - 1))
    twin = (z * 2 + (1 - h), d)
    pair = (e, (d + ndp // 2) % ndp)

    def near_peer(k):
        return (e, dx * near + (dy + k) % near)

    def far_peer(k):
        return (e, ((dx + k) % far) * near + dy)

    def remote(src, dst, send, recv, device):
        return pltpu.make_async_remote_copy(
            src_ref=src, dst_ref=dst, send_sem=send, recv_sem=recv, device_id=device, device_id_type=MESH
        )

    def block(index):
        return pl.ds(pl.multiple_of(index * rows, rows), rows)

    def term(a, way, index):
        cols = pl.ds(way * half, half)
        if a == GATE:
            return contract(x_ref[block(index), :], gate_ref[:, cols], 1, 0)
        if a == UP:
            return contract(x_ref[block(index), :], up_ref[:, cols], 1, 0)
        return contract(rows_ref[block(index), :], down_ref[cols, :], 1, 1)

    barrier = pltpu.get_barrier_semaphore()

    def greet(device):
        pl.semaphore_signal(barrier, inc=1, device_id=device, device_id_type=MESH)

    for device in (to[0], to[1], twin):
        greet(device)
    for k in range(1, far):
        greet(far_peer(k))

    def greet_near(k, carry):
        greet(near_peer(k))
        return carry

    lax.fori_loop(1, near, greet_near, 0)

    forward = [(a, way) for a in (GATE, UP) for way in (0, 1)]

    def ring_copy(a, way, s):
        return remote(
            ring.at[a, way, s], ring.at[a, way, s + 1], ring_send.at[a, way, s], ring_recv.at[a, way, s], to[way]
        )

    def chunk(way, s):
        return (z + (nz - 1 - s if way == 0 else 1 + s)) % nz

    for a, way in forward:
        ring[a, way, 0] = term(a, way, chunk(way, 0)).astype(jnp.bfloat16)
    pl.semaphore_wait(barrier, near + far + 1)
    for a, way in forward:
        ring_copy(a, way, 0).start()

    def near_copy(k):
        peer = near_peer(k)
        return remote(placed_ref.at[(dy + k) % near], mid.at[dy], near_send, near_recv, peer)

    def near_start(k, carry):
        near_copy(k).start()
        return carry

    lax.fori_loop(1, near, near_start, 0)
    keep = pltpu.make_async_copy(placed_ref.at[dy], mid.at[dy], local_sem.at[0])
    keep.start()

    def ring_step(s, carry):
        for a, way in forward:
            mine = term(a, way, chunk(way, s + 1))
            ring_copy(a, way, s).wait_recv()
            ring[a, way, s + 1] = (ring[a, way, s + 1].astype(jnp.float32) + mine).astype(jnp.bfloat16)
            ring_copy(a, way, s + 1).start()
        return carry

    lax.fori_loop(0, FIRST, ring_step, 0)

    near_all = remote(
        placed_ref.at[pl.ds(0, near - 1)], mid.at[pl.ds(0, near - 1)], near_send, near_recv, near_peer(1)
    )
    near_all.wait_recv()
    keep.wait()
    far_copies = [
        remote(mid.at[:, (dx + k) % far], arrived.at[dx], far_send.at[k], far_recv.at[k], far_peer(k))
        for k in range(1, far)
    ]
    for copy in far_copies:
        copy.start()
    keep = pltpu.make_async_copy(mid.at[:, dx], arrived.at[dx], local_sem.at[1])
    keep.start()
    x_copy = remote(x_ref, x_other, x_send, x_recv, pair)
    x_copy.start()

    lax.fori_loop(FIRST, SECOND, ring_step, 0)

    for copy in far_copies:
        copy.wait_recv()
    keep.wait()
    rows_ref[...] = arrived[...].astype(jnp.float32).reshape(rows_ref.shape).astype(jnp.bfloat16)

    reach = (nz // 2 - 1, nz // 2)

    def act_copy(way, part, s):
        return remote(
            ring_act.at[way, part, s],
            ring_act.at[way, part, s + 1],
            act_send.at[way, part, s],
            act_recv.at[way, part, s],
            to[way],
        )

    def act_chunk(way, s):
        return (z + (reach[0] - s if way == 0 else nz - reach[1] + s)) % nz

    def act_step(s):
        for part in (0, 1):
            for way in (1, 0):
                if s + 1 < reach[way]:
                    mine = term(ACT, part, act_chunk(way, s + 1))
                    act_copy(way, part, s).wait_recv()
                    ring_act[way, part, s + 1] = (
                        ring_act[way, part, s + 1].astype(jnp.float32) + mine
                    ).astype(jnp.bfloat16)
                    act_copy(way, part, s + 1).start()

    for part in (0, 1):
        for way in (1, 0):
            ring_act[way, part, 0] = term(ACT, part, act_chunk(way, 0)).astype(jnp.bfloat16)
            act_copy(way, part, 0).start()

    def swap_copy(a, way):
        return remote(swap_out.at[a, way], swap_in.at[a, way], swap_send.at[a, way], swap_recv.at[a, way], twin)

    def swap_start(a, way, total):
        own[a, way] = total
        swap_out[a, way] = total.astype(jnp.bfloat16)
        swap_copy(a, way).start()

    act_done = 0
    for s in range(SECOND, nz - 2):
        ring_step(s, 0)
        if act_done < reach[1] - 1:
            act_step(act_done)
            act_done += 1
    for a, way in forward:
        mine = term(a, way, z)
        ring_copy(a, way, nz - 2).wait_recv()
        swap_start(a, way, ring[a, way, nz - 1].astype(jnp.float32) + mine)
    for s in range(act_done, reach[1] - 1):
        act_step(s)
    for part in (0, 1):
        total = term(ACT, part, z)
        for way in (0, 1):
            act_copy(way, part, reach[way] - 1).wait_recv()
            total = total + ring_act[way, part, reach[way]].astype(jnp.float32)
        swap_start(ACT, part, total)

    def full_copy(a, way, s):
        at = block((z + (nz - s if way == 0 else s)) % nz)
        return remote(
            full.at[a, way, at, :], full.at[a, way, at, :], full_send.at[a, way, s], full_recv.at[a, way, s], to[way]
        )

    def other_copy(a, way, s):
        at = block((z + (nz - s if way == 0 else s)) % nz)
        return remote(
            other.at[a, way, at, :],
            other.at[a, way, at, :],
            other_send.at[a, way, s],
            other_recv.at[a, way, s],
            to[way],
        )

    def pair_copy(a, way):
        at = block(z)
        return remote(
            full.at[a, way, at, :], other.at[a, way, at, :], pair_send.at[a, way], pair_recv.at[a, way], pair
        )

    for way in (0, 1):
        value = []
        for a in (GATE, UP, ACT):
            swap_copy(a, way).wait_recv()
            value.append(own[a, way] + swap_in[a, way].astype(jnp.float32))
        gate_pre, up_pre, grad_act = value
        sigmoid_gate = jax.nn.sigmoid(gate_pre)
        gated = gate_pre * sigmoid_gate
        full[ACT, way, block(z), :] = (gated * up_pre).astype(jnp.bfloat16)
        full_copy(ACT, way, 0).start()
        full[GATE, way, block(z), :] = (
            grad_act * up_pre * sigmoid_gate * (1.0 + gate_pre * (1.0 - sigmoid_gate))
        ).astype(jnp.bfloat16)
        full_copy(GATE, way, 0).start()
        full[UP, way, block(z), :] = (grad_act * gated).astype(jnp.bfloat16)
        full_copy(UP, way, 0).start()
        pair_copy(GATE, way).start()
        pair_copy(UP, way).start()

    def full_step(s, carry):
        for a in (ACT, GATE, UP):
            for way in (0, 1):
                full_copy(a, way, s).wait_recv()
                full_copy(a, way, s + 1).start()
        return carry

    lax.fori_loop(0, nz - 2, full_step, 0)

    for a in (GATE, UP):
        for way in (0, 1):
            pair_copy(a, way).wait_recv()
            other_copy(a, way, 0).start()

    for a in (GATE, UP):
        for way in (0, 1):
            full_copy(a, way, nz - 2).wait_recv()
    going[...] = (
        sum(
            contract(full[a, way], w[:, pl.ds(way * half, half)], 1, 1)
            for a, w in ((GATE, gate_ref), (UP, up_ref))
            for way in (0, 1)
        )
        .reshape(going.shape)
        .astype(jnp.bfloat16)
    )
    back_far = [
        remote(
            going.at[(dx + k) % far], mid_back.at[dx], back_far_send.at[k], back_far_recv.at[k], far_peer(k)
        )
        for k in range(1, far)
    ]
    for copy in back_far:
        copy.start()
    keep = pltpu.make_async_copy(going.at[dx], mid_back.at[dx], local_sem.at[2])
    keep.start()

    down_copy = [
        remote(down_out.at[way], down_in.at[way], down_send.at[way], down_recv.at[way], pair) for way in (0, 1)
    ]

    def down_part(way):
        full_copy(ACT, way, nz - 2).wait_recv()
        part = contract(full[ACT, way], rows_ref[...], 0, 0)
        grad_down_ref[pl.ds(way * half, half), :] = part.astype(jnp.bfloat16)
        down_out[way] = part.astype(jnp.bfloat16)
        down_copy[way].start()

    def other_step(s, carry):
        for a in (GATE, UP):
            for way in (0, 1):
                other_copy(a, way, s).wait_recv()
                other_copy(a, way, s + 1).start()
        return carry

    other_step(0, 0)
    down_part(0)
    other_step(1, 0)
    down_part(1)
    lax.fori_loop(2, 4, other_step, 0)

    for copy in back_far:
        copy.wait_recv()
    keep.wait()

    def back_copy(k):
        return remote(
            mid_back.at[:, (dy + k) % near], back.at[dy], back_near_send, back_near_recv, near_peer(k)
        )

    def back_start(k, carry):
        back_copy(k).start()
        return carry

    lax.fori_loop(1, near, back_start, 0)
    keep = pltpu.make_async_copy(mid_back.at[:, dy], back.at[dy], local_sem.at[3])
    keep.start()
    lax.fori_loop(4, nz - 2, other_step, 0)

    x_copy.wait_recv()
    shared = shared_ref[0:1, 0:1]
    for a, out in ((GATE, grad_gate_ref), (UP, grad_up_ref)):
        for way in (0, 1):
            part = contract(x_ref[...], full[a, way], 0, 0)
            other_copy(a, way, nz - 2).wait_recv()
            part = part + shared * contract(x_other[...], other[a, way], 0, 0)
            out[:, pl.ds(way * half, half)] = part.astype(jnp.bfloat16)

    everything_back = remote(
        back.at[pl.ds(0, near - 1)], back.at[pl.ds(0, near - 1)], back_near_send, back_near_recv, near_peer(1)
    )
    everything_back.wait_recv()
    keep.wait()
    came = back[...].astype(jnp.float32).reshape(rows_ref.shape).astype(jnp.bfloat16)
    grad_input_ref[...] = contract(pick_ref[...], came, 1, 0).astype(jnp.bfloat16)

    for way in (0, 1):
        at = pl.ds(way * half, half)
        down_copy[way].wait_recv()
        grad_down_ref[at, :] = (
            grad_down_ref[at, :].astype(jnp.float32) + shared * down_in[way].astype(jnp.float32)
        ).astype(jnp.bfloat16)

    near_all.wait_send()
    everything_back.wait_send()
    for copy in far_copies + back_far:
        copy.wait_send()
    x_copy.wait_send()
    for way in (0, 1):
        down_copy[way].wait_send()
        for a in (GATE, UP, ACT):
            swap_copy(a, way).wait_send()
        for a in (GATE, UP):
            pair_copy(a, way).wait_send()
        for part in (0, 1):
            for s in range(reach[way]):
                act_copy(way, part, s).wait_send()

    def drain(s, carry):
        for way in (0, 1):
            for a in (GATE, UP):
                ring_copy(a, way, s).wait_send()
                other_copy(a, way, s).wait_send()
            for a in (GATE, UP, ACT):
                full_copy(a, way, s).wait_send()
        return carry

    lax.fori_loop(0, nz - 1, drain, 0)


def slot_call(shared, x, placed, pick, gate_w, up_w, down_w):
    nz = lax.axis_size("expert") // 2
    count, width = x.shape
    hidden = gate_w.shape[1]
    half = hidden // 2
    part = count // nz
    near, far, capacity, _ = placed.shape
    bf16, f32 = jnp.bfloat16, jnp.float32
    vmem = pl.BlockSpec(memory_space=pltpu.VMEM)
    dma = pltpu.SemaphoreType.DMA
    return pl.pallas_call(
        slot_kernel,
        out_shape=(
            jax.ShapeDtypeStruct((pick.shape[0], width), bf16),
            jax.ShapeDtypeStruct((width, hidden), bf16),
            jax.ShapeDtypeStruct((width, hidden), bf16),
            jax.ShapeDtypeStruct((hidden, width), bf16),
        ),
        in_specs=[vmem] * 7,
        out_specs=(vmem,) * 4,
        scratch_shapes=[
            pltpu.VMEM((near, far, capacity, width), bf16),
            pltpu.VMEM((far, near, capacity, width), bf16),
            pltpu.VMEM((count, width), bf16),
            pltpu.VMEM((far, near, capacity, width), bf16),
            pltpu.VMEM((far, near, capacity, width), bf16),
            pltpu.VMEM((near, far, capacity, width), bf16),
            pltpu.VMEM((2, 2, nz, part, half), bf16),
            pltpu.VMEM((2, 2, nz // 2 + 1, part, half), bf16),
            pltpu.VMEM((3, 2, part, half), f32),
            pltpu.VMEM((3, 2, part, half), bf16),
            pltpu.VMEM((3, 2, part, half), bf16),
            pltpu.VMEM((3, 2, count, half), bf16),
            pltpu.VMEM((2, 2, count, half), bf16),
            pltpu.VMEM((count, width), bf16),
            pltpu.VMEM((2, half, width), bf16),
            pltpu.VMEM((2, half, width), bf16),
            dma,
            dma,
            dma((far,)),
            dma((far,)),
            dma((far,)),
            dma((far,)),
            dma,
            dma,
            dma((4,)),
            dma((2, 2, nz - 1)),
            dma((2, 2, nz - 1)),
            dma((2, 2, nz // 2)),
            dma((2, 2, nz // 2)),
            dma((3, 2)),
            dma((3, 2)),
            dma((3, 2, nz - 1)),
            dma((3, 2, nz - 1)),
            dma((2, 2, nz - 1)),
            dma((2, 2, nz - 1)),
            dma((2, 2)),
            dma((2, 2)),
            dma,
            dma,
            dma((2,)),
            dma((2,)),
        ],
        compiler_params=pltpu.CompilerParams(
            collective_id=0, has_side_effects=True, vmem_limit_bytes=40 * 1024 * 1024
        ),
    )(shared, x, placed, pick, gate_w, up_w, down_w)


def local(
    grad_out, gate_prob, routes, slot_expert, saved_input, gate_weight, up_weight, down_weight
):
    tok_rows, width_part = grad_out.shape
    fanout = routes.shape[1]
    slot_count = lax.axis_size("dp")
    capacity = saved_input.shape[1] // slot_count
    far = FAR
    near = slot_count // far
    flat_routes = routes.reshape(-1)
    chosen = (flat_routes[:, None] == jnp.arange(slot_count, dtype=jnp.int32)[None, :]).astype(
        jnp.int32
    )
    earlier = jnp.cumsum(chosen, axis=0) - chosen
    position = jnp.sum(earlier * chosen, axis=1)
    target = ((flat_routes % near) * far + flat_routes // near) * capacity + position
    slots = jnp.arange(slot_count * capacity, dtype=jnp.int32)
    select = (slots[:, None] == target[None, :]).astype(jnp.bfloat16)
    pick = jnp.sum(
        (target.reshape(tok_rows, fanout, 1) == slots[None, None, :]).astype(jnp.float32), axis=1
    ).astype(jnp.bfloat16)
    scaled = (gate_prob[:, :, None] * grad_out[:, None, :].astype(jnp.float32)).astype(jnp.bfloat16)
    scaled = scaled.reshape(tok_rows * fanout, width_part)
    placed = jnp.dot(select, scaled, preferred_element_type=jnp.float32).astype(jnp.bfloat16)
    my_slot = lax.axis_index("dp")
    partner = (my_slot + slot_count // 2) % slot_count
    shared = (slot_expert[my_slot] == slot_expert[partner]).astype(jnp.float32)
    grad_input, grad_gate_w, grad_up_w, grad_down_w = slot_call(
        jnp.full((8, 128), shared, jnp.float32),
        saved_input[0],
        placed.reshape(near, far, capacity, width_part),
        pick,
        gate_weight[0],
        up_weight[0],
        down_weight[0],
    )
    return (grad_input, grad_gate_w[None], grad_up_w[None], grad_down_w[None])


def solution(mesh):
    placed = (
        P("dp", "expert"),
        P("dp", None),
        P("dp", None),
        P(),
        P("dp", None, "expert"),
        P("dp", "expert", None),
        P("dp", "expert", None),
        P("dp", None, "expert"),
    )
    return jax.shard_map(
        local,
        mesh=mesh,
        in_specs=placed,
        out_specs=(
            P("dp", "expert"),
            P("dp", "expert", None),
            P("dp", "expert", None),
            P("dp", None, "expert"),
        ),
        check_vma=False,
    )
```

```python
import jax
import jax.numpy as jnp
from jax import lax
from jax.experimental import pallas as pl
from jax.experimental.pallas import tpu as pltpu
from jax.sharding import PartitionSpec as P

MESH = pl.DeviceIdType.MESH
GATE, UP, ACT = 0, 1, 2
OTHER = 3
FAR = 4


def contract(left, right, left_dim, right_dim):
    return lax.dot_general(
        left, right, (((left_dim,), (right_dim,)), ((), ())), preferred_element_type=jnp.float32
    )


def slot_kernel(
    routes_ref,
    prob_ref,
    grad_out_ref,
    expert_ref,
    x_hbm,
    gate_hbm,
    up_hbm,
    down_hbm,
    grad_input_ref,
    grad_gate_ref,
    grad_up_ref,
    grad_down_ref,
    x_ref,
    gate_ref,
    up_ref,
    down_ref,
    pick_ref,
    placed_ref,
    mid,
    arrived,
    rows_ref,
    going,
    mid_back,
    back,
    ring,
    own,
    swap_out,
    swap_in,
    full,
    other,
    x_other,
    x_turned,
    part_own,
    down_out,
    down_in,
    load_sem,
    near_send,
    near_recv,
    far_send,
    far_recv,
    back_far_send,
    back_far_recv,
    back_near_send,
    back_near_recv,
    local_sem,
    ring_send,
    ring_recv,
    swap_send,
    swap_recv,
    full_send,
    full_recv,
    pair_send,
    pair_recv,
    x_send,
    x_recv,
    down_send,
    down_recv,
):
    e = lax.axis_index("expert")
    d = lax.axis_index("dp")
    nz = lax.axis_size("expert") // 2
    ndp = lax.axis_size("dp")
    far, near = mid.shape[1], mid.shape[0]
    dx, dy = d // near, d % near
    z, h = e // 2, e % 2
    rows = x_ref.shape[0] // nz
    half = gate_ref.shape[1] // 2
    to = tuple((((z + k) % nz) * 2 + h, d) for k in (1, nz - 1))
    twin = (z * 2 + (1 - h), d)
    pair = (e, (d + ndp // 2) % ndp)

    def near_peer(k):
        return (e, dx * near + (dy + k) % near)

    def far_peer(k):
        return (e, ((dx + k) % far) * near + dy)

    def remote(src, dst, send, recv, device):
        return pltpu.make_async_remote_copy(
            src_ref=src, dst_ref=dst, send_sem=send, recv_sem=recv, device_id=device, device_id_type=MESH
        )

    def block(index):
        return pl.ds(pl.multiple_of(index * rows, rows), rows)

    def term(a, way, index):
        cols = pl.ds(way * half, half)
        if a == GATE:
            return contract(x_ref[block(index), :], gate_ref[:, cols], 1, 0)
        if a == UP:
            return contract(x_ref[block(index), :], up_ref[:, cols], 1, 0)
        return contract(rows_ref[block(index), :], down_ref[cols, :], 1, 1)

    loads = [
        pltpu.make_async_copy(src, dst, load_sem.at[i])
        for i, (src, dst) in enumerate(
            ((x_hbm, x_ref), (gate_hbm, gate_ref), (up_hbm, up_ref), (down_hbm, down_ref))
        )
    ]
    for load in loads:
        load.start()

    barrier = pltpu.get_barrier_semaphore()

    def greet(device):
        pl.semaphore_signal(barrier, inc=1, device_id=device, device_id_type=MESH)

    for device in (to[0], to[1], twin):
        greet(device)
    for k in range(1, far):
        greet(far_peer(k))

    def greet_near(k, carry):
        greet(near_peer(k))
        return carry

    lax.fori_loop(1, near, greet_near, 0)

    capacity = placed_ref.shape[2]
    shape = (near * far * capacity, routes_ref.shape[1])
    line = lax.broadcasted_iota(jnp.int32, shape, 0)
    group = lax.div(line, capacity)
    slot = lax.rem(group, far) * near + lax.div(group, far)
    chosen = jnp.zeros(shape, jnp.float32)
    weight = jnp.zeros(shape, jnp.float32)
    for k in range(routes_ref.shape[0]):
        same = routes_ref[k : k + 1, :] == slot
        chosen = jnp.where(same, 1.0, chosen)
        weight = jnp.where(same, prob_ref[k : k + 1, :], weight)
    tokens = (shape[1], shape[1])
    before = jnp.where(
        lax.broadcasted_iota(jnp.int32, tokens, 0) < lax.broadcasted_iota(jnp.int32, tokens, 1), 1.0, 0.0
    ).astype(jnp.bfloat16)
    earlier = contract(chosen.astype(jnp.bfloat16), before, 1, 0)
    pick = jnp.where(earlier == lax.rem(line, capacity).astype(jnp.float32), chosen, 0.0)
    pick_ref[...] = pick.astype(jnp.bfloat16)
    scale = jnp.sum(pick * weight, axis=1, keepdims=True)
    placed = scale * contract(pick.astype(jnp.bfloat16), grad_out_ref[...], 1, 0)
    placed_ref[...] = placed.reshape(placed_ref.shape).astype(jnp.bfloat16)

    reach = nz // 2

    def ring_copy(a, way, part, s):
        return remote(
            ring.at[a, way, part, s],
            ring.at[a, way, part, s + 1],
            ring_send.at[a, way, part, s],
            ring_recv.at[a, way, part, s],
            to[way],
        )

    def ring_term(a, way, part, s):
        return term(a, part, (z + (reach - s if way == 0 else nz - reach + s)) % nz)

    def ring_start(a, way):
        for part, s in ((way, 0), (1 - way, 1)):
            ring[a, way, part, s] = ring_term(a, way, part, s).astype(jnp.bfloat16)

    def ring_send_first(a, way):
        for part, s in ((way, 0), (1 - way, 1)):
            ring_copy(a, way, part, s).start()

    def ring_step(a, i):
        for ahead in (0, 1):
            s = i + ahead
            if s + 1 < reach:
                for way in (0, 1):
                    part = way if ahead == 0 else 1 - way
                    mine = ring_term(a, way, part, s + 1)
                    ring_copy(a, way, part, s).wait_recv()
                    ring[a, way, part, s + 1] = (
                        ring[a, way, part, s + 1].astype(jnp.float32) + mine
                    ).astype(jnp.bfloat16)
                    ring_copy(a, way, part, s + 1).start()

    def ring_end(a):
        for part in (0, 1):
            total = term(a, part, z)
            for way in (0, 1):
                ring_copy(a, way, part, reach - 1).wait_recv()
                total = total + ring[a, way, part, reach].astype(jnp.float32)
            own[a, part] = total
            swap_out[a, part] = total.astype(jnp.bfloat16)
            swap_copy(a, part).start()

    def swap_copy(a, way):
        return remote(swap_out.at[a, way], swap_in.at[a, way], swap_send.at[a, way], swap_recv.at[a, way], twin)

    for load in loads[:3]:
        load.wait()
    for a in (GATE, UP):
        for way in (0, 1):
            ring_start(a, way)
    pl.semaphore_wait(barrier, near + far + 1)

    def near_copy(k):
        peer = near_peer(k)
        return remote(placed_ref.at[(dy + k) % near], mid.at[dy], near_send, near_recv, peer)

    def near_start(k, carry):
        near_copy(k).start()
        return carry

    lax.fori_loop(1, near, near_start, 0)
    for a in (GATE, UP):
        for way in (0, 1):
            ring_send_first(a, way)
    keep = pltpu.make_async_copy(placed_ref.at[dy], mid.at[dy], local_sem.at[0])
    keep.start()

    ring_step(GATE, 0)
    ring_step(UP, 0)

    near_all = remote(
        placed_ref.at[pl.ds(0, near - 1)], mid.at[pl.ds(0, near - 1)], near_send, near_recv, near_peer(1)
    )
    near_all.wait_recv()
    keep.wait()
    far_copies = [
        remote(mid.at[:, (dx + k) % far], arrived.at[dx], far_send.at[k], far_recv.at[k], far_peer(k))
        for k in range(1, far)
    ]
    for copy in far_copies:
        copy.start()
    keep = pltpu.make_async_copy(mid.at[:, dx], arrived.at[dx], local_sem.at[1])
    keep.start()

    ring_step(GATE, 1)
    ring_step(UP, 1)

    for copy in far_copies:
        copy.wait_recv()
    keep.wait()
    loads[3].wait()
    rows_ref[...] = arrived[...].astype(jnp.float32).reshape(rows_ref.shape).astype(jnp.bfloat16)

    for way in (0, 1):
        ring_start(ACT, way)
        ring_send_first(ACT, way)
    ring_step(GATE, 2)
    ring_step(UP, 2)
    ring_step(ACT, 0)
    ring_end(GATE)
    ring_end(UP)
    ring_step(ACT, 1)
    ring_step(ACT, 2)
    ring_end(ACT)

    def gather_copy(a, way, part, s):
        at = block((z + (nz - s if way == 0 else s)) % nz)
        array = full.at[a, part, at, :] if a < 3 else other.at[a - 3, part, at, :]
        return remote(array, array, full_send.at[a, way, part, s], full_recv.at[a, way, part, s], to[way])

    def gather_start(a, part):
        for way in (0, 1):
            gather_copy(a, way, part, 0).start()

    def gather_step(a, s):
        for part in (0, 1):
            for way in (0, 1):
                gather_copy(a, way, part, s).wait_recv()
                if s + 2 < reach or way == part:
                    gather_copy(a, way, part, s + 1).start()

    def gather_end(a, part):
        gather_copy(a, part, part, reach - 1).wait_recv()

    def pair_copy(a, way):
        at = block(z)
        return remote(
            full.at[a, way, at, :], other.at[a, way, at, :], pair_send.at[a, way], pair_recv.at[a, way], pair
        )

    for way in (0, 1):
        value = []
        for a in (GATE, UP, ACT):
            swap_copy(a, way).wait_recv()
            value.append(own[a, way] + swap_in[a, way].astype(jnp.float32))
        gate_pre, up_pre, grad_act = value
        sigmoid_gate = jax.nn.sigmoid(gate_pre)
        gated = gate_pre * sigmoid_gate
        full[ACT, way, block(z), :] = (gated * up_pre).astype(jnp.bfloat16)
        gather_start(ACT, way)
        full[GATE, way, block(z), :] = (
            grad_act * up_pre * sigmoid_gate * (1.0 + gate_pre * (1.0 - sigmoid_gate))
        ).astype(jnp.bfloat16)
        gather_start(GATE, way)
        full[UP, way, block(z), :] = (grad_act * gated).astype(jnp.bfloat16)
    for way in (0, 1):
        pair_copy(GATE, way).start()
        pair_copy(UP, way).start()
    x_copy = remote(x_ref, x_other, x_send, x_recv, pair)
    x_copy.start()
    x_turned[...] = x_ref[...].T

    def down_part(way):
        gather_end(ACT, way)
        part = contract(full[ACT, way], rows_ref[...], 0, 0)
        grad_down_ref[pl.ds(way * half, half), :] = part.astype(jnp.bfloat16)
        down_out[way] = part.astype(jnp.bfloat16)
        down_copy[way].start()

    down_copy = [
        remote(down_out.at[way], down_in.at[way], down_send.at[way], down_recv.at[way], pair) for way in (0, 1)
    ]
    gather_step(ACT, 0)
    gather_step(GATE, 0)
    for part in (0, 1):
        gather_start(UP, part)
    gather_step(ACT, 1)
    gather_step(GATE, 1)
    gather_step(UP, 0)
    gather_step(ACT, 2)
    gather_step(GATE, 2)
    gather_step(UP, 1)
    for a in (GATE, UP):
        for part in (0, 1):
            pair_copy(a, part).wait_recv()
            gather_start(OTHER + a, part)
    down_part(0)
    gather_step(UP, 2)
    down_part(1)
    gather_step(OTHER + GATE, 0)
    gather_step(OTHER + UP, 0)
    for a in (GATE, UP):
        for part in (0, 1):
            gather_end(a, part)
    going[...] = (
        sum(
            contract(full[a, way], w[:, pl.ds(way * half, half)], 1, 1)
            for a, w in ((GATE, gate_ref), (UP, up_ref))
            for way in (0, 1)
        )
        .reshape(going.shape)
        .astype(jnp.bfloat16)
    )
    back_far = [
        remote(
            going.at[(dx + k) % far], mid_back.at[dx], back_far_send.at[k], back_far_recv.at[k], far_peer(k)
        )
        for k in range(1, far)
    ]
    for copy in back_far:
        copy.start()
    keep = pltpu.make_async_copy(going.at[dx], mid_back.at[dx], local_sem.at[2])
    keep.start()

    def own_part(a, way):
        part_own[a, way] = contract(x_turned[...], full[a, way], 1, 0)

    gather_step(OTHER + GATE, 1)
    own_part(GATE, 0)
    gather_step(OTHER + UP, 1)
    own_part(GATE, 1)
    for copy in back_far:
        copy.wait_recv()
    keep.wait()

    def back_copy(k):
        return remote(
            mid_back.at[:, (dy + k) % near], back.at[dy], back_near_send, back_near_recv, near_peer(k)
        )

    def back_start(k, carry):
        back_copy(k).start()
        return carry

    lax.fori_loop(1, near, back_start, 0)
    keep = pltpu.make_async_copy(mid_back.at[:, dy], back.at[dy], local_sem.at[3])
    keep.start()
    gather_step(OTHER + GATE, 2)
    own_part(UP, 0)
    gather_step(OTHER + UP, 2)
    own_part(UP, 1)
    x_copy.wait_recv()
    x_turned[...] = x_other[...].T
    d_line = lax.broadcasted_iota(jnp.int32, expert_ref.shape, 1)
    mine = jnp.sum(jnp.where(d_line == d, expert_ref[...], 0), axis=1, keepdims=True)
    theirs = jnp.sum(jnp.where(d_line == pair[1], expert_ref[...], 0), axis=1, keepdims=True)
    shared = jnp.where(mine == theirs, 1.0, 0.0)
    for a, out in ((GATE, grad_gate_ref), (UP, grad_up_ref)):
        for way in (0, 1):
            gather_end(OTHER + a, way)
            part = part_own[a, way] + shared * contract(x_turned[...], other[a, way], 1, 0)
            out[:, pl.ds(way * half, half)] = part.astype(jnp.bfloat16)

    everything_back = remote(
        back.at[pl.ds(0, near - 1)], back.at[pl.ds(0, near - 1)], back_near_send, back_near_recv, near_peer(1)
    )
    everything_back.wait_recv()
    keep.wait()
    came = back[...].astype(jnp.float32).reshape(rows_ref.shape).astype(jnp.bfloat16)
    grad_input_ref[...] = contract(pick_ref[...], came, 0, 0).astype(jnp.bfloat16)

    for way in (0, 1):
        at = pl.ds(way * half, half)
        down_copy[way].wait_recv()
        grad_down_ref[at, :] = (
            grad_down_ref[at, :].astype(jnp.float32) + shared * down_in[way].astype(jnp.float32)
        ).astype(jnp.bfloat16)

    near_all.wait_send()
    everything_back.wait_send()
    for copy in far_copies + back_far:
        copy.wait_send()
    x_copy.wait_send()
    for way in (0, 1):
        down_copy[way].wait_send()
        for a in (GATE, UP, ACT):
            swap_copy(a, way).wait_send()
        for a in (GATE, UP):
            pair_copy(a, way).wait_send()

    def drain(part, carry):
        for way in (0, 1):
            for a in range(5):
                for step in range(reach - 1):
                    gather_copy(a, way, part, step).wait_send()
            for a in (GATE, UP, ACT):
                for step in range(1, reach):
                    ring_copy(a, way, part, step).wait_send()
        for a in range(5):
            gather_copy(a, part, part, reach - 1).wait_send()
        for a in (GATE, UP, ACT):
            ring_copy(a, part, part, 0).wait_send()
        return carry

    for part in (0, 1):
        drain(part, 0)


def slot_call(routes, prob, grad_out, expert, x, gate_w, up_w, down_w):
    nz = lax.axis_size("expert") // 2
    count, width = x.shape
    hidden = gate_w.shape[1]
    half = hidden // 2
    part = count // nz
    far = FAR
    near = lax.axis_size("dp") // far
    capacity = count // (near * far)
    tokens = grad_out.shape[0]
    bf16, f32 = jnp.bfloat16, jnp.float32
    vmem = pl.BlockSpec(memory_space=pltpu.VMEM)
    hbm = pl.BlockSpec(memory_space=pl.ANY)
    dma = pltpu.SemaphoreType.DMA
    return pl.pallas_call(
        slot_kernel,
        out_shape=(
            jax.ShapeDtypeStruct((tokens, width), bf16),
            jax.ShapeDtypeStruct((width, hidden), bf16),
            jax.ShapeDtypeStruct((width, hidden), bf16),
            jax.ShapeDtypeStruct((hidden, width), bf16),
        ),
        in_specs=[vmem] * 4 + [hbm] * 4,
        out_specs=(vmem,) * 4,
        scratch_shapes=[
            pltpu.VMEM((count, width), bf16),
            pltpu.VMEM((width, hidden), bf16),
            pltpu.VMEM((width, hidden), bf16),
            pltpu.VMEM((hidden, width), bf16),
            pltpu.VMEM((count, tokens), bf16),
            pltpu.VMEM((near, far, capacity, width), bf16),
            pltpu.VMEM((near, far, capacity, width), bf16),
            pltpu.VMEM((far, near, capacity, width), bf16),
            pltpu.VMEM((count, width), bf16),
            pltpu.VMEM((far, near, capacity, width), bf16),
            pltpu.VMEM((far, near, capacity, width), bf16),
            pltpu.VMEM((near, far, capacity, width), bf16),
            pltpu.VMEM((3, 2, 2, nz // 2 + 1, part, half), bf16),
            pltpu.VMEM((3, 2, part, half), f32),
            pltpu.VMEM((3, 2, part, half), bf16),
            pltpu.VMEM((3, 2, part, half), bf16),
            pltpu.VMEM((3, 2, count, half), bf16),
            pltpu.VMEM((2, 2, count, half), bf16),
            pltpu.VMEM((count, width), bf16),
            pltpu.VMEM((width, count), bf16),
            pltpu.VMEM((2, 2, width, half), f32),
            pltpu.VMEM((2, half, width), bf16),
            pltpu.VMEM((2, half, width), bf16),
            dma((4,)),
            dma,
            dma,
            dma((far,)),
            dma((far,)),
            dma((far,)),
            dma((far,)),
            dma,
            dma,
            dma((4,)),
            dma((3, 2, 2, nz // 2)),
            dma((3, 2, 2, nz // 2)),
            dma((3, 2)),
            dma((3, 2)),
            dma((5, 2, 2, nz // 2)),
            dma((5, 2, 2, nz // 2)),
            dma((2, 2)),
            dma((2, 2)),
            dma,
            dma,
            dma((2,)),
            dma((2,)),
        ],
        compiler_params=pltpu.CompilerParams(
            collective_id=0, has_side_effects=True, vmem_limit_bytes=56 * 1024 * 1024
        ),
    )(routes, prob, grad_out, expert, x, gate_w, up_w, down_w)


def local(
    grad_out, gate_prob, routes, slot_expert, saved_input, gate_weight, up_weight, down_weight
):
    grad_input, grad_gate_w, grad_up_w, grad_down_w = slot_call(
        routes.T,
        gate_prob.T,
        grad_out,
        slot_expert[None],
        saved_input[0],
        gate_weight[0],
        up_weight[0],
        down_weight[0],
    )
    return (grad_input, grad_gate_w[None], grad_up_w[None], grad_down_w[None])


def solution(mesh):
    placed = (
        P("dp", "expert"),
        P("dp", None),
        P("dp", None),
        P(),
        P("dp", None, "expert"),
        P("dp", "expert", None),
        P("dp", "expert", None),
        P("dp", None, "expert"),
    )
    return jax.shard_map(
        local,
        mesh=mesh,
        in_specs=placed,
        out_specs=(
            P("dp", "expert"),
            P("dp", "expert", None),
            P("dp", "expert", None),
            P("dp", None, "expert"),
        ),
        check_vma=False,
    )
```

```python
import jax
import jax.numpy as jnp
from jax import lax
from jax.experimental import pallas as pl
from jax.experimental.pallas import tpu as pltpu
from jax.sharding import PartitionSpec as P

MESH = pl.DeviceIdType.MESH
GATE, UP, ACT = 0, 1, 2
OTHER = 3
FAR = 4


def contract(left, right, left_dim, right_dim):
    return lax.dot_general(
        left, right, (((left_dim,), (right_dim,)), ((), ())), preferred_element_type=jnp.float32
    )


def slot_kernel(
    routes_ref,
    prob_ref,
    grad_out_ref,
    expert_ref,
    x_hbm,
    gate_hbm,
    up_hbm,
    down_hbm,
    grad_input_ref,
    grad_gate_ref,
    grad_up_ref,
    grad_down_ref,
    x_ref,
    gate_ref,
    up_ref,
    down_ref,
    pick_ref,
    placed_ref,
    mid,
    arrived,
    rows_ref,
    going,
    mid_back,
    back,
    ring,
    own,
    swap_out,
    swap_in,
    full,
    other,
    x_other,
    x_turned,
    part_own,
    down_out,
    down_in,
    load_sem,
    near_send,
    near_recv,
    far_send,
    far_recv,
    back_far_send,
    back_far_recv,
    back_near_send,
    back_near_recv,
    local_sem,
    ring_send,
    ring_recv,
    swap_send,
    swap_recv,
    twin_send,
    twin_recv,
    full_send,
    full_recv,
    pair_send,
    pair_recv,
    x_send,
    x_recv,
    down_send,
    down_recv,
):
    e = lax.axis_index("expert")
    d = lax.axis_index("dp")
    nz = lax.axis_size("expert") // 2
    ndp = lax.axis_size("dp")
    far, near = mid.shape[1], mid.shape[0]
    dx, dy = d // near, d % near
    z, h = e // 2, e % 2
    rows = x_ref.shape[0] // nz
    half = gate_ref.shape[1] // 2
    to = tuple((((z + k) % nz) * 2 + h, d) for k in (1, nz - 1))
    twin = (z * 2 + (1 - h), d)
    pair = (e, (d + ndp // 2) % ndp)

    def near_peer(k):
        return (e, dx * near + (dy + k) % near)

    def far_peer(k):
        return (e, ((dx + k) % far) * near + dy)

    def remote(src, dst, send, recv, device):
        return pltpu.make_async_remote_copy(
            src_ref=src, dst_ref=dst, send_sem=send, recv_sem=recv, device_id=device, device_id_type=MESH
        )

    def block(index):
        return pl.ds(pl.multiple_of(index * rows, rows), rows)

    few = rows // 2

    def lot(index):
        return pl.ds(pl.multiple_of(index * few, few), few)

    def term(a, way, index):
        cols = pl.ds(way * half, half)
        if a == GATE:
            return contract(x_ref[block(index), :], gate_ref[:, cols], 1, 0)
        if a == UP:
            return contract(x_ref[block(index), :], up_ref[:, cols], 1, 0)
        return contract(rows_ref[block(index), :], down_ref[cols, :], 1, 1)

    loads = [
        pltpu.make_async_copy(src, dst, load_sem.at[i])
        for i, (src, dst) in enumerate(
            ((x_hbm, x_ref), (gate_hbm, gate_ref), (up_hbm, up_ref), (down_hbm, down_ref))
        )
    ]
    for load in loads:
        load.start()

    barrier = pltpu.get_barrier_semaphore()

    def greet(device):
        pl.semaphore_signal(barrier, inc=1, device_id=device, device_id_type=MESH)

    for device in (to[0], to[1], twin):
        greet(device)
    for k in range(1, far):
        greet(far_peer(k))

    def greet_near(k, carry):
        greet(near_peer(k))
        return carry

    lax.fori_loop(1, near, greet_near, 0)

    capacity = placed_ref.shape[2]
    shape = (near * far * capacity, routes_ref.shape[1])
    line = lax.broadcasted_iota(jnp.int32, shape, 0)
    group = lax.div(line, capacity)
    slot = lax.rem(group, far) * near + lax.div(group, far)
    chosen = jnp.zeros(shape, jnp.float32)
    weight = jnp.zeros(shape, jnp.float32)
    for k in range(routes_ref.shape[0]):
        same = routes_ref[k : k + 1, :] == slot
        chosen = jnp.where(same, 1.0, chosen)
        weight = jnp.where(same, prob_ref[k : k + 1, :], weight)
    tokens = (shape[1], shape[1])
    before = jnp.where(
        lax.broadcasted_iota(jnp.int32, tokens, 0) < lax.broadcasted_iota(jnp.int32, tokens, 1), 1.0, 0.0
    ).astype(jnp.bfloat16)
    earlier = contract(chosen.astype(jnp.bfloat16), before, 1, 0)
    pick = jnp.where(earlier == lax.rem(line, capacity).astype(jnp.float32), chosen, 0.0)
    pick_ref[...] = pick.astype(jnp.bfloat16)
    scale = jnp.sum(pick * weight, axis=1, keepdims=True)
    placed = scale * contract(pick.astype(jnp.bfloat16), grad_out_ref[...], 1, 0)
    placed_ref[...] = placed.reshape(placed_ref.shape).astype(jnp.bfloat16)

    reach = nz // 2

    def ring_copy(a, way, part, s):
        return remote(
            ring.at[a, way, part, s],
            ring.at[a, way, part, s + 1],
            ring_send.at[a, way, part, s],
            ring_recv.at[a, way, part, s],
            to[way],
        )

    def ring_term(a, way, part, s):
        return term(a, part, (z + (reach - s if way == 0 else nz - reach + s)) % nz)

    def ring_start(a, way):
        for part, s in ((way, 0), (1 - way, 1)):
            ring[a, way, part, s] = ring_term(a, way, part, s).astype(jnp.bfloat16)

    def ring_send_first(a, way):
        for part, s in ((way, 0), (1 - way, 1)):
            ring_copy(a, way, part, s).start()

    def ring_step(a, i):
        for ahead in (0, 1):
            s = i + ahead
            if s + 1 < reach:
                for way in (0, 1):
                    part = way if ahead == 0 else 1 - way
                    mine = ring_term(a, way, part, s + 1)
                    ring_copy(a, way, part, s).wait_recv()
                    ring[a, way, part, s + 1] = (
                        ring[a, way, part, s + 1].astype(jnp.float32) + mine
                    ).astype(jnp.bfloat16)
                    ring_copy(a, way, part, s + 1).start()

    def ring_end(a):
        for part in (0, 1):
            total = term(a, part, z)
            for way in (0, 1):
                ring_copy(a, way, part, reach - 1).wait_recv()
                total = total + ring[a, way, part, reach].astype(jnp.float32)
            own[a, part] = total
            swap_out[a, part] = total.astype(jnp.bfloat16)
            swap_copy(a, part).start()

    def swap_copy(a, way):
        return remote(
            swap_out.at[a, way, lot(1 - h), :],
            swap_in.at[a, way],
            swap_send.at[a, way],
            swap_recv.at[a, way],
            twin,
        )

    for load in loads[:3]:
        load.wait()
    for a in (GATE, UP):
        for way in (0, 1):
            ring_start(a, way)
    pl.semaphore_wait(barrier, near + far + 1)

    def near_copy(k):
        peer = near_peer(k)
        return remote(placed_ref.at[(dy + k) % near], mid.at[dy], near_send, near_recv, peer)

    def near_start(k, carry):
        near_copy(k).start()
        return carry

    lax.fori_loop(1, near, near_start, 0)
    for a in (GATE, UP):
        for way in (0, 1):
            ring_send_first(a, way)
    keep = pltpu.make_async_copy(placed_ref.at[dy], mid.at[dy], local_sem.at[0])
    keep.start()

    ring_step(GATE, 0)
    ring_step(UP, 0)

    near_all = remote(
        placed_ref.at[pl.ds(0, near - 1)], mid.at[pl.ds(0, near - 1)], near_send, near_recv, near_peer(1)
    )
    near_all.wait_recv()
    keep.wait()
    far_copies = [
        remote(mid.at[:, (dx + k) % far], arrived.at[dx], far_send.at[k], far_recv.at[k], far_peer(k))
        for k in range(1, far)
    ]
    for copy in far_copies:
        copy.start()
    keep = pltpu.make_async_copy(mid.at[:, dx], arrived.at[dx], local_sem.at[1])
    keep.start()

    ring_step(GATE, 1)
    ring_step(UP, 1)

    for copy in far_copies:
        copy.wait_recv()
    keep.wait()
    loads[3].wait()
    rows_ref[...] = arrived[...].astype(jnp.float32).reshape(rows_ref.shape).astype(jnp.bfloat16)

    for way in (0, 1):
        ring_start(ACT, way)
        ring_send_first(ACT, way)
    ring_step(GATE, 2)
    ring_step(UP, 2)
    ring_step(ACT, 0)
    ring_end(GATE)
    ring_end(UP)
    ring_step(ACT, 1)
    ring_step(ACT, 2)
    ring_end(ACT)

    def piece(s, which):
        return lot(s % nz * 2 + (h if which == 0 else 1 - h))

    def gather_copy(a, way, part, s, which):
        at = piece(z + (nz - s if way == 0 else s), which)
        array = full.at[a, part, at, :] if a < 3 else other.at[a - 3, part, at, :]
        return remote(
            array, array, full_send.at[a, which, way, part, s], full_recv.at[a, which, way, part, s], to[way]
        )

    def gather_start(a, part, which):
        for way in (0, 1):
            gather_copy(a, way, part, 0, which).start()

    def gather_step(a, s):
        for which in (0, 1):
            for part in (0, 1):
                for way in (0, 1):
                    gather_copy(a, way, part, s, which).wait_recv()
                    if s + 2 < reach or way == part:
                        gather_copy(a, way, part, s + 1, which).start()

    def gather_end(a, part):
        for which in (0, 1):
            gather_copy(a, part, part, reach - 1, which).wait_recv()

    def twin_copy(a, part):
        array = full.at[a, part, piece(z, 0), :]
        return remote(array, array, twin_send.at[a, part], twin_recv.at[a, part], twin)

    def pair_copy(a, way):
        at = block(z)
        return remote(
            full.at[a, way, at, :], other.at[a, way, at, :], pair_send.at[a, way], pair_recv.at[a, way], pair
        )

    for part in (0, 1):
        value = []
        for a in (GATE, UP, ACT):
            swap_copy(a, part).wait_recv()
            value.append(own[a, part, lot(h), :] + swap_in[a, part].astype(jnp.float32))
        gate_pre, up_pre, grad_act = value
        sigmoid_gate = jax.nn.sigmoid(gate_pre)
        gated = gate_pre * sigmoid_gate
        full[ACT, part, piece(z, 0), :] = (gated * up_pre).astype(jnp.bfloat16)
        twin_copy(ACT, part).start()
        gather_start(ACT, part, 0)
        full[GATE, part, piece(z, 0), :] = (
            grad_act * up_pre * sigmoid_gate * (1.0 + gate_pre * (1.0 - sigmoid_gate))
        ).astype(jnp.bfloat16)
        twin_copy(GATE, part).start()
        gather_start(GATE, part, 0)
        full[UP, part, piece(z, 0), :] = (grad_act * gated).astype(jnp.bfloat16)
        twin_copy(UP, part).start()
        gather_start(UP, part, 0)
    for a in (ACT, GATE):
        for part in (0, 1):
            twin_copy(a, part).wait_recv()
            gather_start(a, part, 1)
            if a != ACT:
                pair_copy(a, part).start()
    x_copy = remote(x_ref, x_other, x_send, x_recv, pair)
    x_copy.start()
    x_turned[...] = x_ref[...].T

    def down_part(way):
        gather_end(ACT, way)
        part = contract(full[ACT, way], rows_ref[...], 0, 0)
        grad_down_ref[pl.ds(way * half, half), :] = part.astype(jnp.bfloat16)
        down_out[way] = part.astype(jnp.bfloat16)
        down_copy[way].start()

    down_copy = [
        remote(down_out.at[way], down_in.at[way], down_send.at[way], down_recv.at[way], pair) for way in (0, 1)
    ]
    gather_step(ACT, 0)
    gather_step(GATE, 0)
    for part in (0, 1):
        twin_copy(UP, part).wait_recv()
        gather_start(UP, part, 1)
        pair_copy(UP, part).start()
    gather_step(ACT, 1)
    gather_step(GATE, 1)
    gather_step(UP, 0)
    gather_step(ACT, 2)
    gather_step(GATE, 2)
    gather_step(UP, 1)
    for a in (GATE, UP):
        for part in (0, 1):
            pair_copy(a, part).wait_recv()
            for which in (0, 1):
                gather_start(OTHER + a, part, which)
    down_part(0)
    gather_step(UP, 2)
    down_part(1)
    gather_step(OTHER + GATE, 0)
    gather_step(OTHER + UP, 0)
    for a in (GATE, UP):
        for part in (0, 1):
            gather_end(a, part)
    going[...] = (
        sum(
            contract(full[a, way], w[:, pl.ds(way * half, half)], 1, 1)
            for a, w in ((GATE, gate_ref), (UP, up_ref))
            for way in (0, 1)
        )
        .reshape(going.shape)
        .astype(jnp.bfloat16)
    )
    back_far = [
        remote(
            going.at[(dx + k) % far], mid_back.at[dx], back_far_send.at[k], back_far_recv.at[k], far_peer(k)
        )
        for k in range(1, far)
    ]
    for copy in back_far:
        copy.start()
    keep = pltpu.make_async_copy(going.at[dx], mid_back.at[dx], local_sem.at[2])
    keep.start()

    def own_part(a, way):
        part_own[a, way] = contract(x_turned[...], full[a, way], 1, 0)

    gather_step(OTHER + GATE, 1)
    own_part(GATE, 0)
    gather_step(OTHER + UP, 1)
    own_part(GATE, 1)
    for copy in back_far:
        copy.wait_recv()
    keep.wait()

    def back_copy(k):
        return remote(
            mid_back.at[:, (dy + k) % near], back.at[dy], back_near_send, back_near_recv, near_peer(k)
        )

    def back_start(k, carry):
        back_copy(k).start()
        return carry

    lax.fori_loop(1, near, back_start, 0)
    keep = pltpu.make_async_copy(mid_back.at[:, dy], back.at[dy], local_sem.at[3])
    keep.start()
    gather_step(OTHER + GATE, 2)
    own_part(UP, 0)
    gather_step(OTHER + UP, 2)
    own_part(UP, 1)
    x_copy.wait_recv()
    x_turned[...] = x_other[...].T
    d_line = lax.broadcasted_iota(jnp.int32, expert_ref.shape, 1)
    mine = jnp.sum(jnp.where(d_line == d, expert_ref[...], 0), axis=1, keepdims=True)
    theirs = jnp.sum(jnp.where(d_line == pair[1], expert_ref[...], 0), axis=1, keepdims=True)
    shared = jnp.where(mine == theirs, 1.0, 0.0)
    def finish(a, out):
        for way in (0, 1):
            gather_end(OTHER + a, way)
            part = part_own[a, way] + shared * contract(x_turned[...], other[a, way], 1, 0)
            out[:, pl.ds(way * half, half)] = part.astype(jnp.bfloat16)

    finish(GATE, grad_gate_ref)
    everything_back = remote(
        back.at[pl.ds(0, near - 1)], back.at[pl.ds(0, near - 1)], back_near_send, back_near_recv, near_peer(1)
    )
    everything_back.wait_recv()
    keep.wait()
    came = back[...].astype(jnp.float32).reshape(rows_ref.shape).astype(jnp.bfloat16)
    grad_input_ref[...] = contract(pick_ref[...], came, 0, 0).astype(jnp.bfloat16)

    for way in (0, 1):
        at = pl.ds(way * half, half)
        down_copy[way].wait_recv()
        grad_down_ref[at, :] = (
            grad_down_ref[at, :].astype(jnp.float32) + shared * down_in[way].astype(jnp.float32)
        ).astype(jnp.bfloat16)

    finish(UP, grad_up_ref)

    near_all.wait_send()
    everything_back.wait_send()
    for copy in far_copies + back_far:
        copy.wait_send()
    x_copy.wait_send()
    for way in (0, 1):
        down_copy[way].wait_send()
        for a in (GATE, UP, ACT):
            swap_copy(a, way).wait_send()
        for a in (GATE, UP):
            pair_copy(a, way).wait_send()

    for part in (0, 1):
        for a in (GATE, UP, ACT):
            twin_copy(a, part).wait_send()
            ring_copy(a, part, part, 0).wait_send()
            for way in (0, 1):
                for step in range(1, reach):
                    ring_copy(a, way, part, step).wait_send()
        for a in range(5):
            for which in (0, 1):
                gather_copy(a, part, part, reach - 1, which).wait_send()
                for way in (0, 1):
                    for step in range(reach - 1):
                        gather_copy(a, way, part, step, which).wait_send()


def slot_call(routes, prob, grad_out, expert, x, gate_w, up_w, down_w):
    nz = lax.axis_size("expert") // 2
    count, width = x.shape
    hidden = gate_w.shape[1]
    half = hidden // 2
    part = count // nz
    far = FAR
    near = lax.axis_size("dp") // far
    capacity = count // (near * far)
    tokens = grad_out.shape[0]
    bf16, f32 = jnp.bfloat16, jnp.float32
    vmem = pl.BlockSpec(memory_space=pltpu.VMEM)
    hbm = pl.BlockSpec(memory_space=pl.ANY)
    dma = pltpu.SemaphoreType.DMA
    return pl.pallas_call(
        slot_kernel,
        out_shape=(
            jax.ShapeDtypeStruct((tokens, width), bf16),
            jax.ShapeDtypeStruct((width, hidden), bf16),
            jax.ShapeDtypeStruct((width, hidden), bf16),
            jax.ShapeDtypeStruct((hidden, width), bf16),
        ),
        in_specs=[vmem] * 4 + [hbm] * 4,
        out_specs=(vmem,) * 4,
        scratch_shapes=[
            pltpu.VMEM((count, width), bf16),
            pltpu.VMEM((width, hidden), bf16),
            pltpu.VMEM((width, hidden), bf16),
            pltpu.VMEM((hidden, width), bf16),
            pltpu.VMEM((count, tokens), bf16),
            pltpu.VMEM((near, far, capacity, width), bf16),
            pltpu.VMEM((near, far, capacity, width), bf16),
            pltpu.VMEM((far, near, capacity, width), bf16),
            pltpu.VMEM((count, width), bf16),
            pltpu.VMEM((far, near, capacity, width), bf16),
            pltpu.VMEM((far, near, capacity, width), bf16),
            pltpu.VMEM((near, far, capacity, width), bf16),
            pltpu.VMEM((3, 2, 2, nz // 2 + 1, part, half), bf16),
            pltpu.VMEM((3, 2, part, half), f32),
            pltpu.VMEM((3, 2, part, half), bf16),
            pltpu.VMEM((3, 2, part // 2, half), bf16),
            pltpu.VMEM((3, 2, count, half), bf16),
            pltpu.VMEM((2, 2, count, half), bf16),
            pltpu.VMEM((count, width), bf16),
            pltpu.VMEM((width, count), bf16),
            pltpu.VMEM((2, 2, width, half), f32),
            pltpu.VMEM((2, half, width), bf16),
            pltpu.VMEM((2, half, width), bf16),
            dma((4,)),
            dma,
            dma,
            dma((far,)),
            dma((far,)),
            dma((far,)),
            dma((far,)),
            dma,
            dma,
            dma((4,)),
            dma((3, 2, 2, nz // 2)),
            dma((3, 2, 2, nz // 2)),
            dma((3, 2)),
            dma((3, 2)),
            dma((3, 2)),
            dma((3, 2)),
            dma((5, 2, 2, 2, nz // 2)),
            dma((5, 2, 2, 2, nz // 2)),
            dma((2, 2)),
            dma((2, 2)),
            dma,
            dma,
            dma((2,)),
            dma((2,)),
        ],
        compiler_params=pltpu.CompilerParams(
            collective_id=0, has_side_effects=True, vmem_limit_bytes=56 * 1024 * 1024
        ),
    )(routes, prob, grad_out, expert, x, gate_w, up_w, down_w)


def local(
    grad_out, gate_prob, routes, slot_expert, saved_input, gate_weight, up_weight, down_weight
):
    grad_input, grad_gate_w, grad_up_w, grad_down_w = slot_call(
        routes.T,
        gate_prob.T,
        grad_out,
        slot_expert[None],
        saved_input[0],
        gate_weight[0],
        up_weight[0],
        down_weight[0],
    )
    return (grad_input, grad_gate_w[None], grad_up_w[None], grad_down_w[None])


def solution(mesh):
    placed = (
        P("dp", "expert"),
        P("dp", None),
        P("dp", None),
        P(),
        P("dp", None, "expert"),
        P("dp", "expert", None),
        P("dp", "expert", None),
        P("dp", None, "expert"),
    )
    return jax.shard_map(
        local,
        mesh=mesh,
        in_specs=placed,
        out_specs=(
            P("dp", "expert"),
            P("dp", "expert", None),
            P("dp", "expert", None),
            P("dp", None, "expert"),
        ),
        check_vma=False,
    )
```
